256 devices in a mesh: grp: 8 (over y, x_hi), blk: 32 (over x_lo, z, core).
Axes of the slice: x: 4 (x_hi: 2, x_lo: 2; x = x_hi * 2 + x_lo), y: 4, z: 8, core: 2. Of those that a mesh axis runs over, the one named last changes fastest.
Arguments:
- large_emb: bfloat16 [98304, 768], P(('grp', 'blk'))
- large_count: int32 [8], P('grp'), may hold values from 6144 to 12288, as said below
- small_emb: bfloat16 [8, 32, 512, 768], P('grp', 'blk')
- small_ids: int32 [8, 32], P('grp', 'blk'), may hold values from 0 to 7
- small_count: int32 [8, 32], P('grp', 'blk'), may hold values from 128 to 512, as said below
Outputs:
- large_max: float32 [98304], P(('grp', 'blk'))
- small_max: float32 [8, 32, 512], P('grp', 'blk')
The draws below stay inside these ranges and needn't reach their ends.
Inputs may be any that keep to these rules, and one draw needn't show every extreme that they name: `large_count`: the live rows of a large cluster are its first rows; at least one cluster is fully live in every draw. `small_count`: the live rows of a block are its first rows; at least one block is fully live in every draw. `small_ids`: ids only matter within one column; equal ids in a column mean one cluster.
All inputs are finite; a program needn't handle non-finite values.
Results may differ from the reference program's by a relative error of at most 0.00059.
Values may be sent and summed in bfloat16 or wider, within the bound.
A program may use at most 128 MiB of HBM per device.

```python
import jax
import jax.numpy as jnp
from jax import lax

D = 768
ROWS_DEV = 384
BR = 512
CL = 12288
N_GRP = 8
N_BLK = 32


def with_partner(key, noise, weight):
    orders = jax.vmap(lambda part_key: jax.random.permutation(part_key, noise.shape[1]))(jax.random.split(key, noise.shape[0]))
    partner = jax.vmap(lambda block, order: block[order])(noise, orders)
    return noise + weight * partner


def draw_large_emb(key, part):
    key = jax.random.fold_in(key, 11)
    keys = jax.random.split(key, 5)
    shape = (N_GRP, CL, D)
    noise = jax.random.normal(keys[0], shape, jnp.float32)
    center = 0.6 * jax.random.normal(keys[1], (N_GRP, 1, D), jnp.float32)
    scale = jnp.exp(jax.random.uniform(keys[2], (N_GRP, CL, 1), jnp.float32, 0.0, 2.4))
    weight = jnp.exp(jax.random.uniform(keys[4], (N_GRP, CL, 1), jnp.float32, -1.6, 1.2))
    rows = scale * (center + with_partner(keys[3], noise, weight))
    return rows.reshape(N_GRP * CL, D).astype(jnp.bfloat16)


def draw_small_emb(key, part):
    key = jax.random.fold_in(key, 37)
    keys = jax.random.split(key, 5)
    shape = (N_BLK, N_GRP * BR, D)
    noise = jax.random.normal(keys[0], shape, jnp.float32)
    center = 0.6 * jax.random.normal(keys[1], (N_BLK, 1, D), jnp.float32)
    scale = jnp.exp(jax.random.uniform(keys[2], (N_BLK, N_GRP * BR, 1), jnp.float32, 0.0, 2.4))
    weight = jnp.exp(jax.random.uniform(keys[4], (N_BLK, N_GRP * BR, 1), jnp.float32, -1.6, 1.2))
    rows = scale * (center + with_partner(keys[3], noise, weight))
    rows = jnp.swapaxes(rows.reshape(N_BLK, N_GRP, BR, D), 0, 1)
    return rows.astype(jnp.bfloat16)


def draw_large_count(key, part):
    key = jax.random.fold_in(key, 23)
    first_key, second_key = jax.random.split(key)
    counts = jax.random.randint(first_key, (N_GRP,), CL // 2, CL + 1)
    full_index = jax.random.randint(second_key, (), 0, N_GRP)
    return jnp.where(jnp.arange(N_GRP) == full_index, CL, counts).astype(jnp.int32)


def draw_small_count(key, part):
    key = jax.random.fold_in(key, 29)
    first_key, second_key = jax.random.split(key)
    counts = jax.random.randint(first_key, (N_GRP * N_BLK,), BR // 4, BR + 1)
    full_index = jax.random.randint(second_key, (), 0, N_GRP * N_BLK)
    counts = jnp.where(jnp.arange(N_GRP * N_BLK) == full_index, BR, counts)
    return counts.reshape(N_GRP, N_BLK).astype(jnp.int32)


def set_ends(values, key, smallest, largest):
    longest = values.shape.index(max(values.shape))
    spots = []
    for shift in (0, 1):
        where = [jax.random.randint(jax.random.fold_in(key, axis), (), 0, length) for axis, length in enumerate(values.shape)]
        where[longest] = (where[longest] + shift) % values.shape[longest]
        spots.append(tuple(where))
    return values.at[spots[0]].set(smallest).at[spots[1]].set(largest)


def setup_inputs(seed: int = 0) -> dict:
    seeds = jax.random.split(jax.random.key(seed), 6)
    return {
        "large_emb": draw_large_emb(jax.random.fold_in(seeds[5], 71), 0),
        "large_count": draw_large_count(jax.random.fold_in(seeds[5], 71), 0),
        "small_emb": draw_small_emb(jax.random.fold_in(seeds[5], 71), 0),
        "small_ids": set_ends(jax.random.randint(seeds[3], (N_GRP, N_BLK), 0, N_GRP), jax.random.fold_in(seeds[3], 1), 0, N_GRP - 1).astype(jnp.int32),
        "small_count": draw_small_count(jax.random.fold_in(seeds[5], 71), 0),
    }


def unit_rows(embedding):
    widened = embedding.astype(jnp.float32)
    inverse = lax.rsqrt(lax.optimization_barrier(jnp.sum(widened * widened, axis=-1, keepdims=True)) + 1e-06)
    return (widened * inverse).astype(jnp.bfloat16)

def reference(large_emb, large_count, small_emb, small_ids, small_count):
    large_unit = unit_rows(large_emb).reshape(N_GRP, CL, D)
    row_index = jnp.arange(CL, dtype=jnp.int32)

    def one_cluster(operands):
        members, live_count = operands

        def query_block(first):
            queries = lax.dynamic_slice_in_dim(members, first, ROWS_DEV, 0)
            query_index = first + jnp.arange(ROWS_DEV, dtype=jnp.int32)
            scores = jnp.dot(queries, members.T, preferred_element_type=jnp.float32)
            valid = (row_index[None, :] < live_count) & (query_index[:, None] != row_index[None, :])
            best_sim = jnp.maximum(lax.optimization_barrier(jnp.max(jnp.where(valid, scores, -2.0), axis=1)), -1.0)
            return jnp.where(query_index < live_count, best_sim, 0.0)
        firsts = jnp.arange(N_BLK, dtype=jnp.int32) * ROWS_DEV
        return lax.map(query_block, firsts).reshape(CL)
    large_max = lax.map(one_cluster, (large_unit, large_count)).reshape(N_GRP * CL)
    small_unit = jnp.swapaxes(unit_rows(small_emb), 0, 1)
    column_ids = small_ids.T
    column_counts = small_count.T
    inner = jnp.arange(BR, dtype=jnp.int32)
    groups = jnp.arange(N_GRP, dtype=jnp.int32)
    key_group = jnp.broadcast_to(groups[:, None], (N_GRP, BR)).reshape(N_GRP * BR)
    key_row = jnp.broadcast_to(inner[None, :], (N_GRP, BR)).reshape(N_GRP * BR)

    def one_column(operands):
        blocks, block_ids, block_counts = operands
        keys = blocks.reshape(N_GRP * BR, D)
        key_live = (inner[None, :] < block_counts[:, None]).reshape(N_GRP * BR)
        key_id = jnp.broadcast_to(block_ids[:, None], (N_GRP, BR)).reshape(N_GRP * BR)

        def one_block(group):
            queries = blocks[group]
            scores = jnp.dot(queries, keys.T, preferred_element_type=jnp.float32)
            same = key_live & (key_id == block_ids[group])
            other = (key_group != group)[None, :] | (inner[:, None] != key_row[None, :])
            valid = same[None, :] & other
            best_sim = jnp.maximum(lax.optimization_barrier(jnp.max(jnp.where(valid, scores, -2.0), axis=1)), -1.0)
            return jnp.where(inner < block_counts[group], best_sim, 0.0)
        return lax.map(one_block, groups)
    small_max = jnp.swapaxes(lax.map(one_column, (small_unit, column_ids, column_counts)), 0, 1)
    return (large_max, small_max)
```

```python
import jax
import jax.numpy as jnp
from jax import lax
from jax.experimental import pallas as pl
from jax.experimental.pallas import tpu as pltpu
from jax.sharding import PartitionSpec as P

EPSILON = 1e-06
MESH = pl.DeviceIdType.MESH
DEAD = -4.0

N_X, N_Y, N_Z = 4, 4, 8
ROWS, D, BR = 384, 768, 512
SUB = 128
PIECES = ((0, 128), (128, 128), (256, 64), (320, 64))
N_PIECE = len(PIECES)
HALF = BR // 2


def unit_rows(embedding):
    widened = embedding.astype(jnp.float32)
    inverse = lax.rsqrt(jnp.sum(widened * widened, axis=-1, keepdims=True) + EPSILON)
    return (widened * inverse).astype(jnp.bfloat16)


def scores_of(rows, cols):
    return lax.dot_general(
        rows, cols, (((1,), (1,)), ((), ())), preferred_element_type=jnp.float32
    )


def over_rows(s):
    m, n = s.shape
    return jnp.max(s.reshape(m // 8, 8, n), axis=0)


def over_cols(s):
    best = s[:, :128]
    for first in range(128, s.shape[1], 128):
        best = jnp.maximum(best, s[:, first : first + 128])
    return best


def turned(best):
    return jnp.concatenate(
        [over_rows(best[f : f + 128].T) for f in range(0, best.shape[0], 128)], axis=1
    )


def add_rows_bias(s, bias):
    return jnp.concatenate(
        [s[:, f : f + 128] + bias for f in range(0, s.shape[1], 128)], axis=1
    )


def kernel(
    large_count, small_id, small_count, large_emb, small_emb,
    large_out, small_out,
    win, far, near, across, meta, meta_across,
    best_win, best_far_rows, best_far, best_near, best_near_rows, best_across,
    got_large, got_small,
    own_s, own_r, fwd_s, fwd_r, sib_s, sib_r, cross_s, cross_r, diag_s, diag_r,
    near_s, near_r, hop_s, hop_r, across_s, across_r, meta_s, meta_r,
    lres_s, lres_r, sres_s, sres_r,
):
    grp, blk = lax.axis_index("grp"), lax.axis_index("blk")
    y, xh = grp // 2, lax.rem(grp, 2)
    c = lax.rem(blk, 2)
    z = lax.rem(blk // 2, N_Z)
    xl = blk // (2 * N_Z)

    def on_z(dz, flip_x=0, flip_c=0):
        z2 = lax.rem(z + dz + N_Z, N_Z)
        x2 = lax.rem(xl + flip_x, 2)
        c2 = lax.rem(c + flip_c, 2)
        return (grp, (x2 * N_Z + z2) * 2 + c2)

    def on_y(dy, flip_x=0):
        return (lax.rem(y + dy + N_Y, N_Y) * 2 + lax.rem(xh + flip_x, 2), blk)

    def remote(src, dst, send, recv, device):
        return pltpu.make_async_remote_copy(
            src_ref=src, dst_ref=dst, send_sem=send, recv_sem=recv,
            device_id=device, device_id_type=MESH,
        )

    wide = xh == c
    thin = xh != c

    partners = [on_z(d) for d in (-2, -1, 1, 2)] + [on_y(d) for d in (-1, 1, 2)]
    partners += [on_y(0, 1), on_z(0, 1, 0), on_z(0, 0, 1)]
    partners += [on_z(d, fx, fc) for d in (-2, 2) for fx, fc in ((0, 1), (1, 0), (1, 1))]
    barrier = pltpu.get_barrier_semaphore()
    for partner in partners:
        pl.semaphore_signal(barrier, inc=1, device_id=partner, device_id_type=MESH)

    def own_copy(i, k):
        rows = pl.ds(PIECES[k][0], PIECES[k][1])
        return remote(win.at[2, rows], win.at[1 + 2 * i, rows], own_s.at[i, k], own_r.at[i, k], on_z(1 - 2 * i))

    def fwd_copy(i, k):
        rows = pl.ds(PIECES[k][0], PIECES[k][1])
        return remote(win.at[1 + 2 * i, rows], win.at[4 * i, rows], fwd_s.at[i, k], fwd_r.at[i, k], on_z(1 - 2 * i))

    def far_rows(kind, k):
        first, n = PIECES[k]
        return far.at[first // SUB, pl.ds(kind * SUB + first % SUB, n)]

    def sib_copy(k):
        rows = pl.ds(PIECES[k][0], PIECES[k][1])
        return remote(win.at[4, rows], far_rows(0, k), sib_s.at[k], sib_r.at[k], on_z(0, 0, 1))

    def cross_copy(k):
        rows = pl.ds(PIECES[k][0], PIECES[k][1])
        return remote(win.at[4, rows], far_rows(1, k), cross_s.at[k], cross_r.at[k], on_z(0, 1, 0))

    def diag_copy(k):
        return remote(far_rows(1, k), far_rows(2, k), diag_s.at[k], diag_r.at[k], on_z(0, 0, 1))

    def near_copy(i, h):
        rows = pl.ds(((1 - i) ^ h) * HALF, HALF)
        return remote(near.at[1, rows], near.at[2 * i, rows], near_s.at[i, h], near_r.at[i, h], on_y(1 - 2 * i))

    def hop_copy(i):
        rows = pl.ds((1 - i) * HALF, HALF)
        return remote(near.at[2 * i, rows], near.at[3, rows], hop_s.at[i], hop_r.at[i], on_y(1 - 2 * i))

    def across_copy():
        return remote(near.at[1], across, across_s.at[0], across_r.at[0], on_y(0, 1))

    def meta_copy(n):
        dst = meta_across if n == 3 else meta.at[(0, 2, 3)[n]]
        return remote(meta.at[1], dst, meta_s.at[n], meta_r.at[n], on_y(0, 1) if n == 3 else on_y((1, -1, 2)[n]))

    def large_result(n):
        src = best_win.at[(0, 1, 3, 4)[n]] if n < 4 else best_far.at[n - 4]
        to = on_z((-2, -1, 1, 2)[n]) if n < 4 else on_z(2, *((0, 1), (1, 0), (1, 1))[n - 4])
        return remote(src, got_large.at[n], lres_s.at[n], lres_r.at[n], to)

    def small_result(n):
        src = best_across if n == 3 else best_near.at[(0, 2, 3)[n]]
        slot = min(n, 2)
        to = on_y(0, 1) if n == 3 else on_y((-1, 1, 2)[n])
        return remote(src, got_small.at[slot], sres_s.at[n], sres_r.at[slot], to)

    for k, (first, n) in enumerate(PIECES):
        win[2, first : first + n] = unit_rows(large_emb[first : first + n])
        if k == 0:
            meta[1] = jnp.full((8, 128), small_id[0, 0] * 1024 + small_count[0, 0], jnp.int32)
            pl.semaphore_wait(barrier, len(partners))
        for i in range(2):
            own_copy(i, k).start()
    for n in range(4):
        meta_copy(n).start()
    for h in (1, 0):
        near[1, h * HALF : (h + 1) * HALF] = unit_rows(small_emb[h * HALF : (h + 1) * HALF])
        near_copy(1 - h, 0).start()
    for i in range(2):
        near_copy(i, 1).start()

    @pl.when(thin)
    def _():
        across_copy().start()

    best_win[...] = jnp.full(best_win.shape, -1.0, jnp.float32)
    best_far_rows[...] = jnp.full(best_far_rows.shape, -1.0, jnp.float32)
    best_near[...] = jnp.full(best_near.shape, -1.0, jnp.float32)
    best_near_rows[...] = jnp.full(best_near_rows.shape, -1.0, jnp.float32)

    count = large_count[0]

    def first_position(dz, flip_x=0, flip_c=0):
        return on_z(dz, flip_x, flip_c)[1] * ROWS

    def col_bias(slot):
        z2 = lax.rem(z + slot - 2 + N_Z, N_Z)
        first = ((xl * N_Z + z2) * 2 + c) * ROWS
        at = first + lax.broadcasted_iota(jnp.int32, (1, ROWS), 1)
        return jnp.where(at < count, 0.0, DEAD)

    def row_bias(first, n):
        at = first + lax.broadcasted_iota(jnp.int32, (n, 128), 0)
        return jnp.where(at < count, 0.0, DEAD)

    def far_bias(k):
        return jnp.concatenate(
            [row_bias(first_position(2, fx, fc) + k * SUB, SUB) for fx, fc in ((0, 1), (1, 0), (1, 1))], axis=0
        )

    def pair(rows, bias, slot):
        s = scores_of(rows, win[slot])
        best_win[slot] = jnp.maximum(best_win[slot], over_rows(add_rows_bias(s, bias)))
        return over_cols(s + col_bias(slot))

    def win_pairs(slot, lowest, n):
        for f in range(0, ROWS, SUB):
            rows = win[slot, f : f + SUB]
            bias = row_bias(first_position(slot - 2) + f, SUB)

            def step(j, best):
                return jnp.maximum(best, pair(rows, bias, lowest + j))

            best = lax.fori_loop(0, n, step, jnp.full((SUB, 128), -1.0, jnp.float32))
            best_win[slot, :, f : f + SUB] = jnp.maximum(best_win[slot, :, f : f + SUB], turned(best))

    def far_pairs(k, lowest, n):
        bias = far_bias(k)

        def step(j, carry):
            best = pair(far[k], bias, lowest + j)
            best_far_rows[k] = jnp.maximum(best_far_rows[k], best)
            return carry

        lax.fori_loop(0, n, step, 0)

    def far_ends(k):
        bias = far_bias(k)
        for f, n, slot in ((0, SUB, 4 - 4 * c), (SUB, 2 * SUB, 4 - 4 * xl)):
            best = pair(far[k, f : f + n], bias[f : f + n], slot)
            best_far_rows[k, f : f + n] = jnp.maximum(best_far_rows[k, f : f + n], best)

    def far_done(k):
        best = turned(best_far_rows[k])
        for kind in range(3):
            best_far[kind, :, k * SUB : (k + 1) * SUB] = best[:, kind * SUB : (kind + 1) * SUB]

    def large_self():
        s = scores_of(win[2], win[2])
        r = lax.broadcasted_iota(jnp.int32, s.shape, 0)
        q = lax.broadcasted_iota(jnp.int32, s.shape, 1)
        s = add_rows_bias(jnp.where(r == q, DEAD, s), row_bias(first_position(0), ROWS))
        best_win[2] = jnp.maximum(best_win[2], over_rows(s))

    def small_col_bias(meta_row, meta_col, first, n):
        at = first + lax.broadcasted_iota(jnp.int32, (1, n), 1)
        r = jnp.concatenate([meta_row[0:1]] * (n // 128), axis=1)
        q = jnp.concatenate([meta_col[0:1]] * (n // 128), axis=1)
        return jnp.where(((r >> 10) == (q >> 10)) & (at < (q & 1023)), 0.0, DEAD)

    def small_row_bias(meta_row, meta_col, first, n):
        at = first + lax.broadcasted_iota(jnp.int32, (n, 128), 0)
        r, q = meta_row[0:1], meta_col[0:1]
        live = jnp.where((r >> 10) == (q >> 10), r & 1023, 0)
        return jnp.where(at < live, 0.0, DEAD)

    def small_self():
        for f in range(0, BR, HALF):
            s = scores_of(near[1, f : f + HALF], near[1])
            r = f + lax.broadcasted_iota(jnp.int32, s.shape, 0)
            q = lax.broadcasted_iota(jnp.int32, s.shape, 1)
            bias = small_row_bias(meta[1], meta[1], f, HALF)
            s = add_rows_bias(jnp.where(r == q, DEAD, s), bias)
            best_near[1] = jnp.maximum(best_near[1], over_rows(s))

    def one_above():
        def step(h, carry):
            f = pl.multiple_of(h * HALF, HALF)
            s = scores_of(near[2, pl.ds(f, HALF)], near[1])
            rb = small_row_bias(meta[2], meta[1], f, HALF)
            cb = small_col_bias(meta[2], meta[1], 0, BR)
            best_near[1] = jnp.maximum(best_near[1], over_rows(add_rows_bias(s, rb)))
            best_near_rows[0, pl.ds(f, HALF)] = jnp.maximum(best_near_rows[0, pl.ds(f, HALF)], over_cols(s + cb))
            return carry

        lax.fori_loop(0, 2, step, 0)

    def two_apart():
        low = 1 - y // 2

        def step(h, carry):
            fr = pl.multiple_of((h * low + (1 - low)) * HALF, HALF)
            fc = pl.multiple_of(h * (1 - low) * HALF, HALF)
            s = scores_of(near[2, pl.ds(fr, HALF)], near[0, pl.ds(fc, HALF)])
            rb = small_row_bias(meta[2], meta[0], fr, HALF)
            cb = small_col_bias(meta[2], meta[0], fc, HALF)
            best_near[0, :, pl.ds(fc, HALF)] = jnp.maximum(
                best_near[0, :, pl.ds(fc, HALF)], over_rows(add_rows_bias(s, rb))
            )
            best_near_rows[0, pl.ds(fr, HALF)] = jnp.maximum(best_near_rows[0, pl.ds(fr, HALF)], over_cols(s + cb))
            return carry

        lax.fori_loop(0, 2, step, 0)

    def with_across(lowest, n):
        def step(j, carry):
            slot = lowest + j // 2
            f = pl.multiple_of(lax.rem(j, 2) * HALF, HALF)
            s = scores_of(across[pl.ds(f, HALF)], near[slot])
            rb = small_row_bias(meta_across[...], meta[slot], f, HALF)
            cb = small_col_bias(meta_across[...], meta[slot], 0, BR)
            best_near[slot] = jnp.maximum(best_near[slot], over_rows(add_rows_bias(s, rb)))
            best_near_rows[1, pl.ds(f, HALF)] = jnp.maximum(best_near_rows[1, pl.ds(f, HALF)], over_cols(s + cb))
            return carry

        lax.fori_loop(0, 2 * n, step, 0)

    large_self()
    for n in range(4):
        meta_copy(n).wait_recv()
    small_self()
    for k in range(N_PIECE):
        for i in range(2):
            own_copy(i, k).wait_recv()
            fwd_copy(i, k).start()
        if k == 1:
            for i in range(2):
                near_copy(i, 0).wait_recv()

            @pl.when(wide)
            def _():
                for i in range(2):
                    hop_copy(i).start()
                across_copy().wait_recv()
                with_across(1, 1)

    win_pairs(3, 1, 2)

    def take(k):
        fwd_copy(1, k).wait_recv()
        sib_copy(k).start()
        cross_copy(k).start()

    def pass_on(k):
        cross_copy(k).wait_recv()
        diag_copy(k).start()

    take(0)
    for i in range(2):
        near_copy(i, 1).wait_recv()
    one_above()
    two_apart()

    @pl.when(wide)
    def _():
        with_across(0, 1)
        with_across(2, 1)

    take(1)
    pass_on(0)

    @pl.when(wide)
    def _():
        for i in range(2):
            hop_copy(i).wait_recv()
        with_across(3, 1)
        best_across[...] = turned(best_near_rows[1])
    best_near[2] = jnp.maximum(best_near[2], turned(best_near_rows[0]))
    for n in range(2):
        small_result(n).start()

    @pl.when(wide)
    def _():
        for n in (2, 3):
            small_result(n).start()

    sib_copy(0).wait_recv()
    diag_copy(0).wait_recv()
    far_pairs(0, 1, 3)
    take(2)
    pass_on(1)
    sib_copy(1).wait_recv()
    diag_copy(1).wait_recv()
    far_pairs(1, 1, 3)
    take(3)
    pass_on(2)
    for k in range(N_PIECE):
        fwd_copy(0, k).wait_recv()
    win_pairs(4, 0, 2)
    for k in range(2):
        far_ends(k)
        far_done(k)
    pass_on(3)
    for k in (2, 3):
        sib_copy(k).wait_recv()
        diag_copy(k).wait_recv()
    far_pairs(2, 1, 3)
    far_ends(2)
    far_done(2)

    for n in range(7):
        large_result(n).start()
    at = lax.broadcasted_iota(jnp.int32, (1, BR), 1)
    for n in range(3):
        small_result(n).wait_recv()
    best = best_near[1]
    for n in range(3):
        best = jnp.maximum(best, got_small[n])
    small_out[...] = jnp.where(at < small_count[0, 0], jnp.max(best, axis=0, keepdims=True), 0.0)
    at = first_position(0) + lax.broadcasted_iota(jnp.int32, (1, ROWS), 1)
    for n in range(7):
        large_result(n).wait_recv()
    best = best_win[2]
    for n in range(7):
        best = jnp.maximum(best, got_large[n])
    large_out[...] = jnp.where(at < count, jnp.max(best, axis=0, keepdims=True), 0.0)

    for k in range(N_PIECE):
        for i in range(2):
            own_copy(i, k).wait_send()
            fwd_copy(i, k).wait_send()
        sib_copy(k).wait_send()
        cross_copy(k).wait_send()
        diag_copy(k).wait_send()
    for i in range(2):
        for h in range(2):
            near_copy(i, h).wait_send()
    for n in range(4):
        meta_copy(n).wait_send()
    for n in range(7):
        large_result(n).wait_send()
    for n in range(2):
        small_result(n).wait_send()

    @pl.when(wide)
    def _():
        for i in range(2):
            hop_copy(i).wait_send()
        for n in (2, 3):
            small_result(n).wait_send()

    @pl.when(thin)
    def _():
        across_copy().wait_send()


def body(large_emb, large_count, small_emb, small_ids, small_count):
    vmem = pl.BlockSpec(memory_space=pltpu.VMEM)
    smem = pl.BlockSpec(memory_space=pltpu.SMEM)
    dma = pltpu.SemaphoreType.DMA
    f32, bf16, i32 = jnp.float32, jnp.bfloat16, jnp.int32
    large, small = pl.pallas_call(
        kernel,
        out_shape=(jax.ShapeDtypeStruct((1, ROWS), f32), jax.ShapeDtypeStruct((1, BR), f32)),
        in_specs=[smem, smem, smem, vmem, vmem],
        out_specs=(vmem, vmem),
        scratch_shapes=[
            pltpu.VMEM((5, ROWS, D), bf16),
            pltpu.VMEM((ROWS // SUB, 3 * SUB, D), bf16),
            pltpu.VMEM((4, BR, D), bf16),
            pltpu.VMEM((BR, D), bf16),
            pltpu.VMEM((4, 8, 128), i32),
            pltpu.VMEM((8, 128), i32),
            pltpu.VMEM((5, 8, ROWS), f32),
            pltpu.VMEM((ROWS // SUB, 3 * SUB, 128), f32),
            pltpu.VMEM((3, 8, ROWS), f32),
            pltpu.VMEM((4, 8, BR), f32),
            pltpu.VMEM((2, BR, 128), f32),
            pltpu.VMEM((8, BR), f32),
            pltpu.VMEM((7, 8, ROWS), f32),
            pltpu.VMEM((3, 8, BR), f32),
            dma((2, N_PIECE)), dma((2, N_PIECE)), dma((2, N_PIECE)), dma((2, N_PIECE)),
            dma((N_PIECE,)), dma((N_PIECE,)), dma((N_PIECE,)), dma((N_PIECE,)), dma((N_PIECE,)), dma((N_PIECE,)),
            dma((2, 2)), dma((2, 2)), dma((2,)), dma((2,)), dma((1,)), dma((1,)), dma((4,)), dma((4,)),
            dma((7,)), dma((7,)), dma((4,)), dma((3,)),
        ],
        compiler_params=pltpu.CompilerParams(
            collective_id=0, has_side_effects=True, vmem_limit_bytes=48 * 2**20
        ),
        name="cluster_maxima",
    )(large_count, small_ids, small_count, large_emb, small_emb.reshape(BR, D))
    return large.reshape(ROWS), small.reshape(1, 1, BR)


def solution(mesh):
    placed = (
        P(("grp", "blk"), None),
        P("grp"),
        P("grp", "blk", None, None),
        P("grp", "blk"),
        P("grp", "blk"),
    )
    return jax.shard_map(
        body,
        mesh=mesh,
        in_specs=placed,
        out_specs=(P(("grp", "blk")), P("grp", "blk", None)),
        check_vma=False,
    )
```

```python
import jax
import jax.numpy as jnp
from jax import lax
from jax.experimental import pallas as pl
from jax.experimental.pallas import tpu as pltpu
from jax.sharding import PartitionSpec as P

EPSILON = 1e-06
MESH = pl.DeviceIdType.MESH
DEAD = -4.0

N_X, N_Y, N_Z = 4, 4, 8
ROWS, D, BR = 384, 768, 512
SUB = 128
PIECES = ((0, 128), (128, 128), (256, 128))
N_PIECE = len(PIECES)
HALF = BR // 2
PLACE = {1: 0, 0: 1, -1: 2, -2: 3, 2: 4}
KINDS = ((0, 1), (1, 0), (1, 1))


def unit_rows(embedding):
    widened = embedding.astype(jnp.float32)
    inverse = lax.rsqrt(jnp.sum(widened * widened, axis=-1, keepdims=True) + EPSILON)
    return (widened * inverse).astype(jnp.bfloat16)


def scores_of(rows, cols):
    return lax.dot_general(
        rows, cols, (((1,), (1,)), ((), ())), preferred_element_type=jnp.float32
    )


def over_rows(s):
    m, n = s.shape
    return jnp.max(s.reshape(m // 8, 8, n), axis=0)


def over_cols(s):
    best = s[:, :128]
    for first in range(128, s.shape[1], 128):
        best = jnp.maximum(best, s[:, first : first + 128])
    return best


def turned(best):
    return jnp.concatenate(
        [over_rows(best[f : f + 128].T) for f in range(0, best.shape[0], 128)], axis=1
    )


def add_rows_bias(s, bias):
    return jnp.concatenate(
        [s[:, f : f + 128] + bias for f in range(0, s.shape[1], 128)], axis=1
    )


def kernel(
    large_count_in, small_id_in, small_count_in, large_emb, small_emb,
    large_out, small_out,
    raw_large, raw_small,
    win, far, near, across, meta, meta_across, live_cols,
    best_win, best_far_rows, best_far, best_near, best_near_rows, best_across,
    got_large, got_small,
    large_count, small_id, small_count,
    scalar_r, raw_r, own_s, own_r, fwd_s, fwd_r, sib_s, sib_r, cross_s, cross_r, diag_s, diag_r,
    near_s, near_r, hop_s, hop_r, across_s, across_r, meta_s, meta_r,
    lres_s, lres_r, sres_s, sres_r,
):
    grp, blk = lax.axis_index("grp"), lax.axis_index("blk")
    y, xh = grp // 2, lax.rem(grp, 2)
    c = lax.rem(blk, 2)
    z = lax.rem(blk // 2, N_Z)
    xl = blk // (2 * N_Z)

    def on_z(dz, flip_x=0, flip_c=0):
        z2 = lax.rem(z + dz + N_Z, N_Z)
        x2 = lax.rem(xl + flip_x, 2)
        c2 = lax.rem(c + flip_c, 2)
        return (grp, (x2 * N_Z + z2) * 2 + c2)

    def on_y(dy, flip_x=0):
        return (lax.rem(y + dy + N_Y, N_Y) * 2 + lax.rem(xh + flip_x, 2), blk)

    def remote(src, dst, send, recv, device):
        return pltpu.make_async_remote_copy(
            src_ref=src, dst_ref=dst, send_sem=send, recv_sem=recv,
            device_id=device, device_id_type=MESH,
        )

    wide = xh == c
    thin = xh != c

    def raw_copy(n):
        if n < 2:
            rows = pl.ds((0, PIECES[0][1])[n], (PIECES[0][1], ROWS - PIECES[0][1])[n])
            return pltpu.make_async_copy(large_emb.at[rows], raw_large.at[rows], raw_r.at[n])
        return pltpu.make_async_copy(small_emb, raw_small, raw_r.at[n])

    def win_rows(dz, k):
        first, n = PIECES[k]
        return win.at[pl.ds(PLACE[dz] * ROWS + first, n)]

    def own_copy(i, k):
        src = win_rows(0, k) if k else large_emb.at[pl.ds(*PIECES[0])]
        return remote(src, win_rows(2 * i - 1, k), own_s.at[i, k], own_r.at[i, k], on_z(1 - 2 * i))

    def fwd_copy(i, k):
        return remote(win_rows(2 * i - 1, k), win_rows(4 * i - 2, k), fwd_s.at[i, k], fwd_r.at[i, k], on_z(1 - 2 * i))

    def far_rows(kind, k):
        first, n = PIECES[k]
        return far.at[first // SUB, pl.ds(kind * SUB + first % SUB, n)]

    def sib_copy(k):
        return remote(win_rows(2, k), far_rows(0, k), sib_s.at[k], sib_r.at[k], on_z(0, 0, 1))

    def cross_copy(k):
        return remote(win_rows(2, k), far_rows(1, k), cross_s.at[k], cross_r.at[k], on_z(0, 1, 0))

    def diag_copy(k):
        return remote(far_rows(1, k), far_rows(2, k), diag_s.at[k], diag_r.at[k], on_z(0, 0, 1))

    def near_copy(i, h):
        rows = pl.ds(((1 - i) ^ h) * HALF, HALF)
        return remote(near.at[1, rows], near.at[2 * i, rows], near_s.at[i, h], near_r.at[i, h], on_y(1 - 2 * i))

    def hop_copy(i):
        rows = pl.ds((1 - i) * HALF, HALF)
        return remote(near.at[2 * i, rows], near.at[3, rows], hop_s.at[i], hop_r.at[i], on_y(1 - 2 * i))

    def across_copy():
        return remote(near.at[1], across, across_s.at[0], across_r.at[0], on_y(0, 1))

    def meta_copy(n):
        if n == 0:
            return remote(meta.at[1], meta.at[0], meta_s.at[0], meta_r.at[0], on_y(1))
        if n == 1:
            return remote(meta.at[1], meta.at[2], meta_s.at[1], meta_r.at[1], on_y(-1))
        if n == 2:
            return remote(meta.at[1], meta_across, meta_s.at[2], meta_r.at[2], on_y(0, 1))
        return remote(meta.at[0], meta.at[3], meta_s.at[3], meta_r.at[3], on_y(1))

    def large_result(n):
        src = best_far.at[n - 4] if n > 3 else best_win.at[:, pl.ds(PLACE[(-2, -1, 1, 2)[n]] * ROWS, ROWS)]
        to = on_z((-2, -1, 1, 2)[n]) if n < 4 else on_z(2, *KINDS[n - 4])
        return remote(src, got_large.at[n], lres_s.at[n], lres_r.at[n], to)

    def small_result(n):
        src = best_across if n == 3 else best_near.at[(0, 2, 3)[n]]
        slot = min(n, 2)
        to = on_y(0, 1) if n == 3 else on_y((-1, 1, 2)[n])
        return remote(src, got_small.at[slot], sres_s.at[n], sres_r.at[slot], to)

    def scalar_copy(n):
        src, dst = ((large_count_in, large_count), (small_id_in, small_id), (small_count_in, small_count))[n]
        return pltpu.make_async_copy(src, dst, scalar_r.at[n])

    partners = [on_z(-1), on_z(1), on_y(-1), on_y(1), on_y(0, 1), on_z(0, 1, 0), on_z(0, 0, 1)]
    barrier = pltpu.get_barrier_semaphore()
    for partner in partners:
        pl.semaphore_signal(barrier, inc=1, device_id=partner, device_id_type=MESH)
    for n in range(3):
        raw_copy(n).start()
    for n in range(3):
        scalar_copy(n).start()
    pl.semaphore_wait(barrier, len(partners))
    for i in range(2):
        own_copy(i, 0).start()
    own_first = PLACE[0] * ROWS
    for k, (first, n) in enumerate(PIECES):
        if k < 2:
            raw_copy(k).wait()
        win[own_first + first : own_first + first + n] = unit_rows(raw_large[first : first + n])
        if k:
            for i in range(2):
                own_copy(i, k).start()
    for n in range(3):
        scalar_copy(n).wait()
    meta[1] = jnp.full((8, 128), small_id[0, 0] * 1024 + small_count[0, 0], jnp.int32)
    for n in range(3):
        meta_copy(n).start()
    raw_copy(2).wait()
    for h in (1, 0):
        near[1, h * HALF : (h + 1) * HALF] = unit_rows(raw_small[h * HALF : (h + 1) * HALF])
        near_copy(1 - h, 0).start()
    for i in range(2):
        near_copy(i, 1).start()

    @pl.when(thin)
    def _():
        across_copy().start()

    best_win[...] = jnp.full(best_win.shape, -1.0, jnp.float32)
    best_near[...] = jnp.full(best_near.shape, -1.0, jnp.float32)
    best_near_rows[...] = jnp.full(best_near_rows.shape, -1.0, jnp.float32)

    count = large_count[0]

    def first_position(dz, flip_x=0, flip_c=0):
        return on_z(dz, flip_x, flip_c)[1] * ROWS

    for dz, place in PLACE.items():
        at = first_position(dz) + lax.broadcasted_iota(jnp.int32, (1, ROWS), 1)
        live_cols[:, place * ROWS : (place + 1) * ROWS] = jnp.where(at < count, 0.0, DEAD)

    def row_bias(first, n):
        at = first + lax.broadcasted_iota(jnp.int32, (n, 128), 0)
        return jnp.where(at < count, 0.0, DEAD)

    def far_bias(k):
        return jnp.concatenate([row_bias(first_position(2, fx, fc) + k * SUB, SUB) for fx, fc in KINDS], axis=0)

    def pairs(rows, bias, lowest, n):
        cols = slice(lowest * ROWS, (lowest + n) * ROWS)
        s = scores_of(rows, win[cols])
        best_win[:, cols] = jnp.maximum(best_win[:, cols], over_rows(add_rows_bias(s, bias)))
        return over_cols(s + live_cols[:, cols])

    def win_pairs(dz, lowest, n):
        own = slice(PLACE[dz] * ROWS, (PLACE[dz] + 1) * ROWS)
        best = pairs(win[own], row_bias(first_position(dz), ROWS), lowest, n)
        best_win[:, own] = jnp.maximum(best_win[:, own], turned(best))

    def far_pairs(k, lowest, n):
        best = pairs(far[k], far_bias(k), lowest, n)
        best_far_rows[k] = best if lowest == 0 else jnp.maximum(best_far_rows[k], best)

    def far_done(k):
        best = turned(best_far_rows[k])
        for kind in range(3):
            best_far[kind, :, k * SUB : (k + 1) * SUB] = best[:, kind * SUB : (kind + 1) * SUB]

    def large_self():
        own = slice(own_first, own_first + ROWS)
        s = scores_of(win[own], win[own])
        r = lax.broadcasted_iota(jnp.int32, s.shape, 0)
        q = lax.broadcasted_iota(jnp.int32, s.shape, 1)
        s = add_rows_bias(jnp.where(r == q, DEAD, s), row_bias(first_position(0), ROWS))
        best_win[:, own] = jnp.maximum(best_win[:, own], over_rows(s))

    def small_col_bias(meta_row, meta_col, first, n):
        at = first + lax.broadcasted_iota(jnp.int32, (1, n), 1)
        r = jnp.concatenate([meta_row[0:1]] * (n // 128), axis=1)
        q = jnp.concatenate([meta_col[0:1]] * (n // 128), axis=1)
        return jnp.where(((r >> 10) == (q >> 10)) & (at < (q & 1023)), 0.0, DEAD)

    def small_row_bias(meta_row, meta_col, first, n):
        at = first + lax.broadcasted_iota(jnp.int32, (n, 128), 0)
        r, q = meta_row[0:1], meta_col[0:1]
        live = jnp.where((r >> 10) == (q >> 10), r & 1023, 0)
        return jnp.where(at < live, 0.0, DEAD)

    def small_self():
        for f in range(0, BR, HALF):
            s = scores_of(near[1, f : f + HALF], near[1])
            r = f + lax.broadcasted_iota(jnp.int32, s.shape, 0)
            q = lax.broadcasted_iota(jnp.int32, s.shape, 1)
            bias = small_row_bias(meta[1], meta[1], f, HALF)
            s = add_rows_bias(jnp.where(r == q, DEAD, s), bias)
            best_near[1] = jnp.maximum(best_near[1], over_rows(s))

    def one_above():
        def step(h, carry):
            f = pl.multiple_of(h * HALF, HALF)
            s = scores_of(near[2, pl.ds(f, HALF)], near[1])
            rb = small_row_bias(meta[2], meta[1], f, HALF)
            cb = small_col_bias(meta[2], meta[1], 0, BR)
            best_near[1] = jnp.maximum(best_near[1], over_rows(add_rows_bias(s, rb)))
            best_near_rows[0, pl.ds(f, HALF)] = jnp.maximum(best_near_rows[0, pl.ds(f, HALF)], over_cols(s + cb))
            return carry

        lax.fori_loop(0, 2, step, 0)

    def two_apart():
        low = 1 - y // 2

        def step(h, carry):
            fr = pl.multiple_of((h * low + (1 - low)) * HALF, HALF)
            fc = pl.multiple_of(h * (1 - low) * HALF, HALF)
            s = scores_of(near[2, pl.ds(fr, HALF)], near[0, pl.ds(fc, HALF)])
            rb = small_row_bias(meta[2], meta[0], fr, HALF)
            cb = small_col_bias(meta[2], meta[0], fc, HALF)
            best_near[0, :, pl.ds(fc, HALF)] = jnp.maximum(
                best_near[0, :, pl.ds(fc, HALF)], over_rows(add_rows_bias(s, rb))
            )
            best_near_rows[0, pl.ds(fr, HALF)] = jnp.maximum(best_near_rows[0, pl.ds(fr, HALF)], over_cols(s + cb))
            return carry

        lax.fori_loop(0, 2, step, 0)

    def with_across(lowest, n):
        def step(j, carry):
            slot = lowest + j // 2
            f = pl.multiple_of(lax.rem(j, 2) * HALF, HALF)
            s = scores_of(across[pl.ds(f, HALF)], near[slot])
            rb = small_row_bias(meta_across[...], meta[slot], f, HALF)
            cb = small_col_bias(meta_across[...], meta[slot], 0, BR)
            best_near[slot] = jnp.maximum(best_near[slot], over_rows(add_rows_bias(s, rb)))
            best_near_rows[1, pl.ds(f, HALF)] = jnp.maximum(best_near_rows[1, pl.ds(f, HALF)], over_cols(s + cb))
            return carry

        lax.fori_loop(0, 2 * n, step, 0)

    def take(k):
        fwd_copy(1, k).wait_recv()
        cross_copy(k).start()
        sib_copy(k).start()

    def pass_on(k):
        cross_copy(k).wait_recv()
        diag_copy(k).start()

    def arrived(k):
        sib_copy(k).wait_recv()
        diag_copy(k).wait_recv()

    large_self()
    small_self()
    ends = [first + n for first, n in PIECES]
    halves_due = next(k for k in range(N_PIECE) if ends[k] >= 2 * SUB)
    for k in range(N_PIECE):
        for i in range(2):
            own_copy(i, k).wait_recv()
            if k == 0:
                first = PLACE[2 * i - 1] * ROWS
                piece = slice(first, first + PIECES[0][1])
                win[piece] = unit_rows(win[piece])
            fwd_copy(i, k).start()
        if k == halves_due:
            for i in range(2):
                near_copy(i, 0).wait_recv()
            for n in range(3):
                meta_copy(n).wait_recv()

            @pl.when(wide)
            def _():
                for i in range(2):
                    hop_copy(i).start()
                meta_copy(3).start()
                across_copy().wait_recv()
                with_across(1, 1)

    win_pairs(1, 1, 2)

    def small_first():
        for i in range(2):
            near_copy(i, 1).wait_recv()
        one_above()
        two_apart()

        @pl.when(wide)
        def _():
            with_across(0, 1)
            with_across(2, 1)

    def small_last():
        @pl.when(wide)
        def _():
            for i in range(2):
                hop_copy(i).wait_recv()
            meta_copy(3).wait_recv()
            with_across(3, 1)
            best_across[...] = turned(best_near_rows[1])

        best_near[2] = jnp.maximum(best_near[2], turned(best_near_rows[0]))
        for n in range(2):
            small_result(n).start()

        @pl.when(wide)
        def _():
            for n in (2, 3):
                small_result(n).start()

    seen = passed = 0
    for k in range(N_PIECE):
        take(k)
        if ends[k] <= 2 * SUB:
            while passed < k:
                pass_on(passed)
                passed += 1
        if ends[k] == SUB:
            small_first()
        if ends[k] == 2 * SUB:
            small_last()
        while seen < passed - 1:
            arrived(seen)
            seen += 1
            if ends[seen - 1] % SUB == 0:
                far_pairs(ends[seen - 1] // SUB - 1, 0, 3)
    while ends[passed] < ROWS:
        pass_on(passed)
        passed += 1
    while ends[seen] <= 2 * SUB:
        arrived(seen)
        seen += 1
        if ends[seen - 1] % SUB == 0:
            far_pairs(ends[seen - 1] // SUB - 1, 0, 3)
    for k in range(N_PIECE):
        fwd_copy(0, k).wait_recv()
    win_pairs(2, 2, 2)
    far_pairs(0, 3, 2)
    far_done(0)
    pass_on(N_PIECE - 1)
    far_pairs(1, 3, 2)
    far_done(1)
    for k in range(seen, N_PIECE):
        arrived(k)
    far_pairs(2, 0, 5)
    far_done(2)
    for n in range(7):
        large_result(n).start()

    at = lax.broadcasted_iota(jnp.int32, (1, BR), 1)
    for n in range(3):
        small_result(n).wait_recv()
    best = best_near[1]
    for n in range(3):
        best = jnp.maximum(best, got_small[n])
    small_out[...] = jnp.where(at < small_count[0, 0], jnp.max(best, axis=0, keepdims=True), 0.0)
    for k in range(N_PIECE):
        for i in range(2):
            own_copy(i, k).wait_send()
            fwd_copy(i, k).wait_send()
        sib_copy(k).wait_send()
        cross_copy(k).wait_send()
        diag_copy(k).wait_send()
    for i in range(2):
        for h in range(2):
            near_copy(i, h).wait_send()
    for n in range(3):
        meta_copy(n).wait_send()
    for n in range(2):
        small_result(n).wait_send()

    @pl.when(wide)
    def _():
        for i in range(2):
            hop_copy(i).wait_send()
        meta_copy(3).wait_send()
        for n in (2, 3):
            small_result(n).wait_send()

    @pl.when(thin)
    def _():
        across_copy().wait_send()

    at = first_position(0) + lax.broadcasted_iota(jnp.int32, (1, ROWS), 1)
    for n in range(7):
        large_result(n).wait_recv()
    best = best_win[:, own_first : own_first + ROWS]
    for n in range(7):
        best = jnp.maximum(best, got_large[n])
    large_out[...] = jnp.where(at < count, jnp.max(best, axis=0, keepdims=True), 0.0)
    for n in range(7):
        large_result(n).wait_send()


def hand_out(large, small, large_out, small_out):
    large_out[...] = large[...].reshape(ROWS)
    small_out[...] = small[...].reshape(1, 1, BR)


def body(large_emb, large_count, small_emb, small_ids, small_count):
    vmem = pl.BlockSpec(memory_space=pltpu.VMEM)
    dma = pltpu.SemaphoreType.DMA
    f32, bf16, i32 = jnp.float32, jnp.bfloat16, jnp.int32
    large, small = pl.pallas_call(
        kernel,
        out_shape=(jax.ShapeDtypeStruct((1, ROWS), f32), jax.ShapeDtypeStruct((1, BR), f32)),
        in_specs=[pl.BlockSpec(memory_space=pl.ANY)] * 5,
        out_specs=(vmem, vmem),
        scratch_shapes=[
            pltpu.VMEM((ROWS, D), bf16),
            pltpu.VMEM((BR, D), bf16),
            pltpu.VMEM((5 * ROWS, D), bf16),
            pltpu.VMEM((ROWS // SUB, 3 * SUB, D), bf16),
            pltpu.VMEM((4, BR, D), bf16),
            pltpu.VMEM((BR, D), bf16),
            pltpu.VMEM((4, 8, 128), i32),
            pltpu.VMEM((8, 128), i32),
            pltpu.VMEM((1, 5 * ROWS), f32),
            pltpu.VMEM((8, 5 * ROWS), f32),
            pltpu.VMEM((ROWS // SUB, 3 * SUB, 128), f32),
            pltpu.VMEM((3, 8, ROWS), f32),
            pltpu.VMEM((4, 8, BR), f32),
            pltpu.VMEM((2, BR, 128), f32),
            pltpu.VMEM((8, BR), f32),
            pltpu.VMEM((7, 8, ROWS), f32),
            pltpu.VMEM((3, 8, BR), f32),
            pltpu.SMEM((1,), i32), pltpu.SMEM((1, 1), i32), pltpu.SMEM((1, 1), i32),
            dma((3,)), dma((3,)), dma((2, N_PIECE)), dma((2, N_PIECE)), dma((2, N_PIECE)), dma((2, N_PIECE)),
            dma((N_PIECE,)), dma((N_PIECE,)), dma((N_PIECE,)), dma((N_PIECE,)), dma((N_PIECE,)), dma((N_PIECE,)),
            dma((2, 2)), dma((2, 2)), dma((2,)), dma((2,)), dma((1,)), dma((1,)), dma((4,)), dma((4,)),
            dma((7,)), dma((7,)), dma((4,)), dma((3,)),
        ],
        compiler_params=pltpu.CompilerParams(
            collective_id=0, has_side_effects=True, vmem_limit_bytes=63_200_000
        ),
        name="cluster_maxima",
    )(large_count, small_ids, small_count, large_emb, small_emb.reshape(BR, D))
    return pl.pallas_call(
        hand_out,
        out_shape=(jax.ShapeDtypeStruct((ROWS,), f32), jax.ShapeDtypeStruct((1, 1, BR), f32)),
        in_specs=[vmem, vmem],
        out_specs=(vmem, vmem),
        name="hand_out",
    )(large, small)


def solution(mesh):
    placed = (
        P(("grp", "blk"), None),
        P("grp"),
        P("grp", "blk", None, None),
        P("grp", "blk"),
        P("grp", "blk"),
    )
    return jax.shard_map(
        body,
        mesh=mesh,
        in_specs=placed,
        out_specs=(P(("grp", "blk")), P("grp", "blk", None)),
        check_vma=False,
    )
```

```python
import jax
import jax.numpy as jnp
from jax import lax
from jax.experimental import pallas as pl
from jax.experimental.pallas import tpu as pltpu
from jax.sharding import PartitionSpec as P

EPSILON = 1e-06
MESH = pl.DeviceIdType.MESH
DEAD = -4.0

N_X, N_Y, N_Z = 4, 4, 8
ROWS, D, BR = 384, 768, 512
SUB = 128
PIECES = ((0, 128), (128, 128), (256, 128))
N_PIECE = len(PIECES)
HALF = BR // 2
PLACE = {1: 0, 0: 1, -1: 2, -2: 3, 2: 4}
KINDS = ((0, 1), (1, 0), (1, 1))


def unit_rows(embedding):
    widened = embedding.astype(jnp.float32)
    inverse = lax.rsqrt(jnp.sum(widened * widened, axis=-1, keepdims=True) + EPSILON)
    return (widened * inverse).astype(jnp.bfloat16)


def scores_of(rows, cols):
    return lax.dot_general(
        rows, cols, (((1,), (1,)), ((), ())), preferred_element_type=jnp.float32
    )


def over_rows(s):
    m, n = s.shape
    return jnp.max(s.reshape(m // 8, 8, n), axis=0)


def over_cols(s):
    best = s[:, :128]
    for first in range(128, s.shape[1], 128):
        best = jnp.maximum(best, s[:, first : first + 128])
    return best


def turned(best):
    return jnp.concatenate(
        [over_rows(best[f : f + 128].T) for f in range(0, best.shape[0], 128)], axis=1
    )


def add_rows_bias(s, bias):
    return jnp.concatenate(
        [s[:, f : f + 128] + bias for f in range(0, s.shape[1], 128)], axis=1
    )


def kernel(
    large_count_in, small_id_in, small_count_in, large_emb, small_emb,
    large_out, small_out,
    raw_large, raw_small,
    win, far, near, across, meta, meta_across, live_cols,
    best_win, best_far_rows, best_far, best_near, best_near_rows, best_across,
    got_large, got_small,
    large_count, small_id, small_count,
    scalar_r, raw_r, own_s, own_r, fwd_s, fwd_r, sib_s, sib_r, cross_s, cross_r, diag_s, diag_r,
    near_s, near_r, hop_s, hop_r, across_s, across_r, meta_s, meta_r,
    lres_s, lres_r, sres_s, sres_r,
):
    grp, blk = lax.axis_index("grp"), lax.axis_index("blk")
    y, xh = grp // 2, lax.rem(grp, 2)
    c = lax.rem(blk, 2)
    z = lax.rem(blk // 2, N_Z)
    xl = blk // (2 * N_Z)

    def on_z(dz, flip_x=0, flip_c=0):
        z2 = lax.rem(z + dz + N_Z, N_Z)
        x2 = lax.rem(xl + flip_x, 2)
        c2 = lax.rem(c + flip_c, 2)
        return (grp, (x2 * N_Z + z2) * 2 + c2)

    def on_y(dy, flip_x=0):
        return (lax.rem(y + dy + N_Y, N_Y) * 2 + lax.rem(xh + flip_x, 2), blk)

    def remote(src, dst, send, recv, device):
        return pltpu.make_async_remote_copy(
            src_ref=src, dst_ref=dst, send_sem=send, recv_sem=recv,
            device_id=device, device_id_type=MESH,
        )

    wide = xh == c
    thin = xh != c

    def raw_copy(n):
        if n < 2:
            rows = pl.ds((0, PIECES[0][1])[n], (PIECES[0][1], ROWS - PIECES[0][1])[n])
            return pltpu.make_async_copy(large_emb.at[rows], raw_large.at[rows], raw_r.at[n])
        return pltpu.make_async_copy(small_emb, raw_small, raw_r.at[n])

    def win_rows(dz, k):
        first, n = PIECES[k]
        return win.at[pl.ds(PLACE[dz] * ROWS + first, n)]

    def own_copy(i, k):
        src = win_rows(0, k) if k else large_emb.at[pl.ds(*PIECES[0])]
        return remote(src, win_rows(2 * i - 1, k), own_s.at[i, k], own_r.at[i, k], on_z(1 - 2 * i))

    def fwd_copy(i, k):
        return remote(win_rows(2 * i - 1, k), win_rows(4 * i - 2, k), fwd_s.at[i, k], fwd_r.at[i, k], on_z(1 - 2 * i))

    def far_rows(kind, k):
        first, n = PIECES[k]
        return far.at[first // SUB, pl.ds(kind * SUB + first % SUB, n)]

    def sib_copy(k):
        return remote(win_rows(2, k), far_rows(0, k), sib_s.at[k], sib_r.at[k], on_z(0, 0, 1))

    def cross_copy(k):
        return remote(win_rows(2, k), far_rows(1, k), cross_s.at[k], cross_r.at[k], on_z(0, 1, 0))

    def diag_copy(k):
        return remote(far_rows(1, k), far_rows(2, k), diag_s.at[k], diag_r.at[k], on_z(0, 0, 1))

    def near_copy(i, h):
        rows = pl.ds(((1 - i) ^ h) * HALF, HALF)
        return remote(near.at[1, rows], near.at[2 * i, rows], near_s.at[i, h], near_r.at[i, h], on_y(1 - 2 * i))

    def hop_copy(i):
        rows = pl.ds((1 - i) * HALF, HALF)
        return remote(near.at[2 * i, rows], near.at[3, rows], hop_s.at[i], hop_r.at[i], on_y(1 - 2 * i))

    def across_copy():
        return remote(near.at[1], across, across_s.at[0], across_r.at[0], on_y(0, 1))

    def meta_copy(n):
        if n == 0:
            return remote(meta.at[1], meta.at[0], meta_s.at[0], meta_r.at[0], on_y(1))
        if n == 1:
            return remote(meta.at[1], meta.at[2], meta_s.at[1], meta_r.at[1], on_y(-1))
        if n == 2:
            return remote(meta.at[1], meta_across, meta_s.at[2], meta_r.at[2], on_y(0, 1))
        return remote(meta.at[0], meta.at[3], meta_s.at[3], meta_r.at[3], on_y(1))

    def large_result(n):
        src = best_far.at[n - 4] if n > 3 else best_win.at[:, pl.ds(PLACE[(-2, -1, 1, 2)[n]] * ROWS, ROWS)]
        to = on_z((-2, -1, 1, 2)[n]) if n < 4 else on_z(2, *KINDS[n - 4])
        return remote(src, got_large.at[n], lres_s.at[n], lres_r.at[n], to)

    def small_result(n):
        src = best_across if n == 3 else best_near.at[(0, 2, 3)[n]]
        slot = min(n, 2)
        to = on_y(0, 1) if n == 3 else on_y((-1, 1, 2)[n])
        return remote(src, got_small.at[slot], sres_s.at[n], sres_r.at[slot], to)

    def scalar_copy(n):
        src, dst = ((large_count_in, large_count), (small_id_in, small_id), (small_count_in, small_count))[n]
        return pltpu.make_async_copy(src, dst, scalar_r.at[n])

    partners = [on_z(-1), on_z(1), on_y(-1), on_y(1), on_y(0, 1), on_z(0, 1, 0), on_z(0, 0, 1)]
    barrier = pltpu.get_barrier_semaphore()
    for partner in partners:
        pl.semaphore_signal(barrier, inc=1, device_id=partner, device_id_type=MESH)
    for n in range(3):
        raw_copy(n).start()
    for n in range(3):
        scalar_copy(n).start()
    pl.semaphore_wait(barrier, len(partners))
    for i in range(2):
        own_copy(i, 0).start()
    own_first = PLACE[0] * ROWS
    for k, (first, n) in enumerate(PIECES):
        if k < 2:
            raw_copy(k).wait()
        win[own_first + first : own_first + first + n] = unit_rows(raw_large[first : first + n])
        if k:
            for i in range(2):
                own_copy(i, k).start()
    for n in range(3):
        scalar_copy(n).wait()
    meta[1] = jnp.full((8, 128), small_id[0, 0] * 1024 + small_count[0, 0], jnp.int32)
    for n in range(3):
        meta_copy(n).start()
    raw_copy(2).wait()
    for h in (1, 0):
        near[1, h * HALF : (h + 1) * HALF] = unit_rows(raw_small[h * HALF : (h + 1) * HALF])
        near_copy(1 - h, 0).start()
    for i in range(2):
        near_copy(i, 1).start()

    @pl.when(thin)
    def _():
        across_copy().start()

    best_win[...] = jnp.full(best_win.shape, -1.0, jnp.float32)
    best_near[...] = jnp.full(best_near.shape, -1.0, jnp.float32)
    best_near_rows[...] = jnp.full(best_near_rows.shape, -1.0, jnp.float32)

    count = large_count[0]

    def first_position(dz, flip_x=0, flip_c=0):
        return on_z(dz, flip_x, flip_c)[1] * ROWS

    for dz, place in PLACE.items():
        at = first_position(dz) + lax.broadcasted_iota(jnp.int32, (1, ROWS), 1)
        live_cols[:, place * ROWS : (place + 1) * ROWS] = jnp.where(at < count, 0.0, DEAD)

    def row_bias(first, n):
        at = first + lax.broadcasted_iota(jnp.int32, (n, 128), 0)
        return jnp.where(at < count, 0.0, DEAD)

    def far_bias(k):
        return jnp.concatenate([row_bias(first_position(2, fx, fc) + k * SUB, SUB) for fx, fc in KINDS], axis=0)

    def pairs(rows, bias, lowest, n):
        cols = slice(lowest * ROWS, (lowest + n) * ROWS)
        s = scores_of(rows, win[cols])
        best_win[:, cols] = jnp.maximum(best_win[:, cols], over_rows(add_rows_bias(s, bias)))
        return over_cols(s + live_cols[:, cols])

    def win_pairs(dz, lowest, n):
        own = slice(PLACE[dz] * ROWS, (PLACE[dz] + 1) * ROWS)
        best = pairs(win[own], row_bias(first_position(dz), ROWS), lowest, n)
        best_win[:, own] = jnp.maximum(best_win[:, own], turned(best))

    def far_pairs(k, lowest, n):
        best = pairs(far[k], far_bias(k), lowest, n)
        best_far_rows[k] = best if lowest == 0 else jnp.maximum(best_far_rows[k], best)

    def far_done(k):
        best = turned(best_far_rows[k])
        for kind in range(3):
            best_far[kind, :, k * SUB : (k + 1) * SUB] = best[:, kind * SUB : (kind + 1) * SUB]

    def large_self():
        own = slice(own_first, own_first + ROWS)
        s = scores_of(win[own], win[own])
        r = lax.broadcasted_iota(jnp.int32, s.shape, 0)
        q = lax.broadcasted_iota(jnp.int32, s.shape, 1)
        s = add_rows_bias(jnp.where(r == q, DEAD, s), row_bias(first_position(0), ROWS))
        best_win[:, own] = jnp.maximum(best_win[:, own], over_rows(s))

    def small_col_bias(meta_row, meta_col, first, n):
        at = first + lax.broadcasted_iota(jnp.int32, (1, n), 1)
        r = jnp.concatenate([meta_row[0:1]] * (n // 128), axis=1)
        q = jnp.concatenate([meta_col[0:1]] * (n // 128), axis=1)
        return jnp.where(((r >> 10) == (q >> 10)) & (at < (q & 1023)), 0.0, DEAD)

    def small_row_bias(meta_row, meta_col, first, n):
        at = first + lax.broadcasted_iota(jnp.int32, (n, 128), 0)
        r, q = meta_row[0:1], meta_col[0:1]
        live = jnp.where((r >> 10) == (q >> 10), r & 1023, 0)
        return jnp.where(at < live, 0.0, DEAD)

    def small_self():
        for f in range(0, BR, HALF):
            s = scores_of(near[1, f : f + HALF], near[1])
            r = f + lax.broadcasted_iota(jnp.int32, s.shape, 0)
            q = lax.broadcasted_iota(jnp.int32, s.shape, 1)
            bias = small_row_bias(meta[1], meta[1], f, HALF)
            s = add_rows_bias(jnp.where(r == q, DEAD, s), bias)
            best_near[1] = jnp.maximum(best_near[1], over_rows(s))

    def one_above():
        def step(h, carry):
            f = pl.multiple_of(h * HALF, HALF)
            s = scores_of(near[2, pl.ds(f, HALF)], near[1])
            rb = small_row_bias(meta[2], meta[1], f, HALF)
            cb = small_col_bias(meta[2], meta[1], 0, BR)
            best_near[1] = jnp.maximum(best_near[1], over_rows(add_rows_bias(s, rb)))
            best_near_rows[0, pl.ds(f, HALF)] = jnp.maximum(best_near_rows[0, pl.ds(f, HALF)], over_cols(s + cb))
            return carry

        lax.fori_loop(0, 2, step, 0)

    def two_apart():
        low = 1 - y // 2

        def step(h, carry):
            fr = pl.multiple_of((h * low + (1 - low)) * HALF, HALF)
            fc = pl.multiple_of(h * (1 - low) * HALF, HALF)
            s = scores_of(near[2, pl.ds(fr, HALF)], near[0, pl.ds(fc, HALF)])
            rb = small_row_bias(meta[2], meta[0], fr, HALF)
            cb = small_col_bias(meta[2], meta[0], fc, HALF)
            best_near[0, :, pl.ds(fc, HALF)] = jnp.maximum(
                best_near[0, :, pl.ds(fc, HALF)], over_rows(add_rows_bias(s, rb))
            )
            best_near_rows[0, pl.ds(fr, HALF)] = jnp.maximum(best_near_rows[0, pl.ds(fr, HALF)], over_cols(s + cb))
            return carry

        lax.fori_loop(0, 2, step, 0)

    def with_across(lowest, n):
        def step(j, carry):
            slot = lowest + j // 2
            f = pl.multiple_of(lax.rem(j, 2) * HALF, HALF)
            s = scores_of(across[pl.ds(f, HALF)], near[slot])
            rb = small_row_bias(meta_across[...], meta[slot], f, HALF)
            cb = small_col_bias(meta_across[...], meta[slot], 0, BR)
            best_near[slot] = jnp.maximum(best_near[slot], over_rows(add_rows_bias(s, rb)))
            best_near_rows[1, pl.ds(f, HALF)] = jnp.maximum(best_near_rows[1, pl.ds(f, HALF)], over_cols(s + cb))
            return carry

        lax.fori_loop(0, 2 * n, step, 0)

    def take(k):
        fwd_copy(1, k).wait_recv()
        cross_copy(k).start()
        sib_copy(k).start()

    def pass_on(k):
        cross_copy(k).wait_recv()
        diag_copy(k).start()

    def arrived(k):
        sib_copy(k).wait_recv()
        diag_copy(k).wait_recv()

    large_self()
    small_self()
    ends = [first + n for first, n in PIECES]
    halves_due = next(k for k in range(N_PIECE) if ends[k] >= 2 * SUB)
    for k in range(N_PIECE):
        for i in range(2):
            own_copy(i, k).wait_recv()
            if k == 0:
                first = PLACE[2 * i - 1] * ROWS
                piece = slice(first, first + PIECES[0][1])
                win[piece] = unit_rows(win[piece])
            fwd_copy(i, k).start()
        if k == halves_due:
            for i in range(2):
                near_copy(i, 0).wait_recv()
            for n in range(3):
                meta_copy(n).wait_recv()

            @pl.when(wide)
            def _():
                for i in range(2):
                    hop_copy(i).start()
                meta_copy(3).start()
                across_copy().wait_recv()
                with_across(1, 1)

    win_pairs(1, 1, 2)

    def small_first():
        for i in range(2):
            near_copy(i, 1).wait_recv()
        one_above()
        two_apart()

        @pl.when(wide)
        def _():
            with_across(0, 1)
            with_across(2, 1)

    def small_last():
        @pl.when(wide)
        def _():
            for i in range(2):
                hop_copy(i).wait_recv()
            meta_copy(3).wait_recv()
            with_across(3, 1)
            best_across[...] = turned(best_near_rows[1])

        best_near[2] = jnp.maximum(best_near[2], turned(best_near_rows[0]))
        for n in range(2):
            small_result(n).start()

        @pl.when(wide)
        def _():
            for n in (2, 3):
                small_result(n).start()

    seen = passed = 0
    for k in range(N_PIECE):
        take(k)
        if ends[k] <= 2 * SUB:
            while passed < k:
                pass_on(passed)
                passed += 1
        if ends[k] == SUB:
            small_first()
        if ends[k] == 2 * SUB:
            small_last()
        while seen < passed - 2:
            arrived(seen)
            seen += 1
            if ends[seen - 1] % SUB == 0:
                far_pairs(ends[seen - 1] // SUB - 1, 0, 3)
    while ends[passed] < ROWS:
        pass_on(passed)
        passed += 1
    while ends[seen] <= 2 * SUB:
        arrived(seen)
        seen += 1
        if ends[seen - 1] % SUB == 0:
            far_pairs(ends[seen - 1] // SUB - 1, 0, 3)
    for k in range(N_PIECE):
        fwd_copy(0, k).wait_recv()
    win_pairs(2, 2, 2)
    far_pairs(0, 3, 2)
    far_done(0)
    pass_on(N_PIECE - 1)
    far_pairs(1, 3, 2)
    far_done(1)
    for k in range(seen, N_PIECE):
        arrived(k)
    far_pairs(2, 0, 5)
    for n in (0, 3, 1, 2):
        large_result(n).start()
    far_done(2)
    for n in (6, 5, 4):
        large_result(n).start()

    at = lax.broadcasted_iota(jnp.int32, (1, BR), 1)
    for n in range(3):
        small_result(n).wait_recv()
    best = best_near[1]
    for n in range(3):
        best = jnp.maximum(best, got_small[n])
    small_out[...] = jnp.where(at < small_count[0, 0], jnp.max(best, axis=0, keepdims=True), 0.0)
    for k in range(N_PIECE):
        for i in range(2):
            own_copy(i, k).wait_send()
            fwd_copy(i, k).wait_send()
        sib_copy(k).wait_send()
        cross_copy(k).wait_send()
        diag_copy(k).wait_send()
    for i in range(2):
        for h in range(2):
            near_copy(i, h).wait_send()
    for n in range(3):
        meta_copy(n).wait_send()
    for n in range(2):
        small_result(n).wait_send()

    @pl.when(wide)
    def _():
        for i in range(2):
            hop_copy(i).wait_send()
        meta_copy(3).wait_send()
        for n in (2, 3):
            small_result(n).wait_send()

    @pl.when(thin)
    def _():
        across_copy().wait_send()

    at = first_position(0) + lax.broadcasted_iota(jnp.int32, (1, ROWS), 1)
    for n in range(7):
        large_result(n).wait_recv()
    best = best_win[:, own_first : own_first + ROWS]
    for n in range(7):
        best = jnp.maximum(best, got_large[n])
    large_out[...] = jnp.where(at < count, jnp.max(best, axis=0, keepdims=True), 0.0)
    for n in range(7):
        large_result(n).wait_send()


def hand_out(large, small, large_out, small_out):
    large_out[...] = large[...].reshape(ROWS)
    small_out[...] = small[...].reshape(1, 1, BR)


def body(large_emb, large_count, small_emb, small_ids, small_count):
    vmem = pl.BlockSpec(memory_space=pltpu.VMEM)
    dma = pltpu.SemaphoreType.DMA
    f32, bf16, i32 = jnp.float32, jnp.bfloat16, jnp.int32
    large, small = pl.pallas_call(
        kernel,
        out_shape=(jax.ShapeDtypeStruct((1, ROWS), f32), jax.ShapeDtypeStruct((1, BR), f32)),
        in_specs=[pl.BlockSpec(memory_space=pl.ANY)] * 5,
        out_specs=(vmem, vmem),
        scratch_shapes=[
            pltpu.VMEM((ROWS, D), bf16),
            pltpu.VMEM((BR, D), bf16),
            pltpu.VMEM((5 * ROWS, D), bf16),
            pltpu.VMEM((ROWS // SUB, 3 * SUB, D), bf16),
            pltpu.VMEM((4, BR, D), bf16),
            pltpu.VMEM((BR, D), bf16),
            pltpu.VMEM((4, 8, 128), i32),
            pltpu.VMEM((8, 128), i32),
            pltpu.VMEM((1, 5 * ROWS), f32),
            pltpu.VMEM((8, 5 * ROWS), f32),
            pltpu.VMEM((ROWS // SUB, 3 * SUB, 128), f32),
            pltpu.VMEM((3, 8, ROWS), f32),
            pltpu.VMEM((4, 8, BR), f32),
            pltpu.VMEM((2, BR, 128), f32),
            pltpu.VMEM((8, BR), f32),
            pltpu.VMEM((7, 8, ROWS), f32),
            pltpu.VMEM((3, 8, BR), f32),
            pltpu.SMEM((1,), i32), pltpu.SMEM((1, 1), i32), pltpu.SMEM((1, 1), i32),
            dma((3,)), dma((3,)), dma((2, N_PIECE)), dma((2, N_PIECE)), dma((2, N_PIECE)), dma((2, N_PIECE)),
            dma((N_PIECE,)), dma((N_PIECE,)), dma((N_PIECE,)), dma((N_PIECE,)), dma((N_PIECE,)), dma((N_PIECE,)),
            dma((2, 2)), dma((2, 2)), dma((2,)), dma((2,)), dma((1,)), dma((1,)), dma((4,)), dma((4,)),
            dma((7,)), dma((7,)), dma((4,)), dma((3,)),
        ],
        compiler_params=pltpu.CompilerParams(
            collective_id=0, has_side_effects=True, vmem_limit_bytes=63_200_000
        ),
        name="cluster_maxima",
    )(large_count, small_ids, small_count, large_emb, small_emb.reshape(BR, D))
    return pl.pallas_call(
        hand_out,
        out_shape=(jax.ShapeDtypeStruct((ROWS,), f32), jax.ShapeDtypeStruct((1, 1, BR), f32)),
        in_specs=[vmem, vmem],
        out_specs=(vmem, vmem),
        name="hand_out",
    )(large, small)


def solution(mesh):
    placed = (
        P(("grp", "blk"), None),
        P("grp"),
        P("grp", "blk", None, None),
        P("grp", "blk"),
        P("grp", "blk"),
    )
    return jax.shard_map(
        body,
        mesh=mesh,
        in_specs=placed,
        out_specs=(P(("grp", "blk")), P("grp", "blk", None)),
        check_vma=False,
    )
```

```python
import jax
import jax.numpy as jnp
from jax import lax
from jax.experimental import pallas as pl
from jax.experimental.pallas import tpu as pltpu
from jax.sharding import PartitionSpec as P

EPSILON = 1e-06
MESH = pl.DeviceIdType.MESH
DEAD = -4.0

N_X, N_Y, N_Z = 4, 4, 8
ROWS, D, BR = 384, 768, 512
SUB = 128
PIECES = ((0, 128), (128, 128), (256, 128))
N_PIECE = len(PIECES)
HALF = BR // 2
PLACE = {1: 0, 0: 1, -1: 2, -2: 3, 2: 4}
KINDS = ((0, 1), (1, 0), (1, 1))


def unit_rows(embedding):
    widened = embedding.astype(jnp.float32)
    inverse = lax.rsqrt(jnp.sum(widened * widened, axis=-1, keepdims=True) + EPSILON)
    return (widened * inverse).astype(jnp.bfloat16)


def scores_of(rows, cols):
    return lax.dot_general(
        rows, cols, (((1,), (1,)), ((), ())), preferred_element_type=jnp.float32
    )


def over_rows(s):
    m, n = s.shape
    return jnp.max(s.reshape(m // 8, 8, n), axis=0)


def over_cols(s):
    best = s[:, :128]
    for first in range(128, s.shape[1], 128):
        best = jnp.maximum(best, s[:, first : first + 128])
    return best


def turned(best):
    return jnp.concatenate(
        [over_rows(best[f : f + 128].T) for f in range(0, best.shape[0], 128)], axis=1
    )


def add_rows_bias(s, bias):
    return jnp.concatenate(
        [s[:, f : f + 128] + bias for f in range(0, s.shape[1], 128)], axis=1
    )


def kernel(
    large_count_in, small_id_in, small_count_in, large_emb, small_emb,
    large_out, small_out,
    raw_large, raw_small,
    win, far, near, across, meta, meta_across, live_cols,
    best_win, best_far_rows, best_far, best_near, best_near_rows, best_across,
    got_large, got_small,
    large_count, small_id, small_count,
    scalar_r, raw_r, own_s, own_r, fwd_s, fwd_r, sib_s, sib_r, cross_s, cross_r, diag_s, diag_r,
    near_s, near_r, hop_s, hop_r, across_s, across_r, meta_s, meta_r,
    lres_s, lres_r, sres_s, sres_r,
):
    grp, blk = lax.axis_index("grp"), lax.axis_index("blk")
    y, xh = grp // 2, lax.rem(grp, 2)
    c = lax.rem(blk, 2)
    z = lax.rem(blk // 2, N_Z)
    xl = blk // (2 * N_Z)

    def on_z(dz, flip_x=0, flip_c=0):
        z2 = lax.rem(z + dz + N_Z, N_Z)
        x2 = lax.rem(xl + flip_x, 2)
        c2 = lax.rem(c + flip_c, 2)
        return (grp, (x2 * N_Z + z2) * 2 + c2)

    def on_y(dy, flip_x=0):
        return (lax.rem(y + dy + N_Y, N_Y) * 2 + lax.rem(xh + flip_x, 2), blk)

    def remote(src, dst, send, recv, device):
        return pltpu.make_async_remote_copy(
            src_ref=src, dst_ref=dst, send_sem=send, recv_sem=recv,
            device_id=device, device_id_type=MESH,
        )

    wide = xh == c
    thin = xh != c

    def raw_copy(n):
        if n < 2:
            rows = pl.ds((0, PIECES[0][1])[n], (PIECES[0][1], ROWS - PIECES[0][1])[n])
            return pltpu.make_async_copy(large_emb.at[rows], raw_large.at[rows], raw_r.at[n])
        return pltpu.make_async_copy(small_emb, raw_small, raw_r.at[n])

    def win_rows(dz, k):
        first, n = PIECES[k]
        return win.at[pl.ds(PLACE[dz] * ROWS + first, n)]

    def own_copy(i, k):
        src = win_rows(0, k) if k else large_emb.at[pl.ds(*PIECES[0])]
        return remote(src, win_rows(2 * i - 1, k), own_s.at[i, k], own_r.at[i, k], on_z(1 - 2 * i))

    def fwd_copy(i, k):
        return remote(win_rows(2 * i - 1, k), win_rows(4 * i - 2, k), fwd_s.at[i, k], fwd_r.at[i, k], on_z(1 - 2 * i))

    def far_rows(kind, k):
        first, n = PIECES[k]
        return far.at[first // SUB, pl.ds(kind * SUB + first % SUB, n)]

    def sib_copy(k):
        return remote(win_rows(2, k), far_rows(0, k), sib_s.at[k], sib_r.at[k], on_z(0, 0, 1))

    def cross_copy(k):
        return remote(win_rows(2, k), far_rows(1, k), cross_s.at[k], cross_r.at[k], on_z(0, 1, 0))

    def diag_copy(k):
        return remote(far_rows(1, k), far_rows(2, k), diag_s.at[k], diag_r.at[k], on_z(0, 0, 1))

    def near_copy(i, h):
        rows = pl.ds(((1 - i) ^ h) * HALF, HALF)
        return remote(near.at[1, rows], near.at[2 * i, rows], near_s.at[i, h], near_r.at[i, h], on_y(1 - 2 * i))

    def hop_copy(i):
        rows = pl.ds((1 - i) * HALF, HALF)
        return remote(near.at[2 * i, rows], near.at[3, rows], hop_s.at[i], hop_r.at[i], on_y(1 - 2 * i))

    def across_copy():
        return remote(near.at[1], across, across_s.at[0], across_r.at[0], on_y(0, 1))

    def meta_copy(n):
        if n == 0:
            return remote(meta.at[1], meta.at[0], meta_s.at[0], meta_r.at[0], on_y(1))
        if n == 1:
            return remote(meta.at[1], meta.at[2], meta_s.at[1], meta_r.at[1], on_y(-1))
        if n == 2:
            return remote(meta.at[1], meta_across, meta_s.at[2], meta_r.at[2], on_y(0, 1))
        return remote(meta.at[0], meta.at[3], meta_s.at[3], meta_r.at[3], on_y(1))

    def large_result(n):
        src = best_far.at[n - 4] if n > 3 else best_win.at[:, pl.ds(PLACE[(-2, -1, 1, 2)[n]] * ROWS, ROWS)]
        to = on_z((-2, -1, 1, 2)[n]) if n < 4 else on_z(2, *KINDS[n - 4])
        return remote(src, got_large.at[n], lres_s.at[n], lres_r.at[n], to)

    def small_result(n):
        src = best_across if n == 3 else best_near.at[(0, 2, 3)[n]]
        slot = min(n, 2)
        to = on_y(0, 1) if n == 3 else on_y((-1, 1, 2)[n])
        return remote(src, got_small.at[slot], sres_s.at[n], sres_r.at[slot], to)

    def scalar_copy(n):
        src, dst = ((large_count_in, large_count), (small_id_in, small_id), (small_count_in, small_count))[n]
        return pltpu.make_async_copy(src, dst, scalar_r.at[n])

    partners = [on_z(-1), on_z(1), on_y(-1), on_y(1), on_y(0, 1), on_z(0, 1, 0), on_z(0, 0, 1)]
    barrier = pltpu.get_barrier_semaphore()
    for partner in partners:
        pl.semaphore_signal(barrier, inc=1, device_id=partner, device_id_type=MESH)
    for n in range(3):
        raw_copy(n).start()
    for n in range(3):
        scalar_copy(n).start()
    pl.semaphore_wait(barrier, len(partners))
    for i in range(2):
        own_copy(i, 0).start()
    own_first = PLACE[0] * ROWS
    for k, (first, n) in enumerate(PIECES):
        if k < 2:
            raw_copy(k).wait()
        win[own_first + first : own_first + first + n] = unit_rows(raw_large[first : first + n])
        if k:
            for i in range(2):
                own_copy(i, k).start()
    for n in range(3):
        scalar_copy(n).wait()
    meta[1] = jnp.full((8, 128), small_id[0, 0] * 1024 + small_count[0, 0], jnp.int32)
    for n in range(3):
        meta_copy(n).start()
    raw_copy(2).wait()
    for h in (1, 0):
        near[1, h * HALF : (h + 1) * HALF] = unit_rows(raw_small[h * HALF : (h + 1) * HALF])
        near_copy(1 - h, 0).start()
    for i in range(2):
        near_copy(i, 1).start()

    @pl.when(thin)
    def _():
        across_copy().start()

    best_win[...] = jnp.full(best_win.shape, -1.0, jnp.float32)
    best_near[...] = jnp.full(best_near.shape, -1.0, jnp.float32)
    best_near_rows[...] = jnp.full(best_near_rows.shape, -1.0, jnp.float32)

    count = large_count[0]

    def first_position(dz, flip_x=0, flip_c=0):
        return on_z(dz, flip_x, flip_c)[1] * ROWS

    for dz, place in PLACE.items():
        at = first_position(dz) + lax.broadcasted_iota(jnp.int32, (1, ROWS), 1)
        live_cols[:, place * ROWS : (place + 1) * ROWS] = jnp.where(at < count, 0.0, DEAD)

    def row_bias(first, n):
        at = first + lax.broadcasted_iota(jnp.int32, (n, 128), 0)
        return jnp.where(at < count, 0.0, DEAD)

    def far_bias(k):
        return jnp.concatenate([row_bias(first_position(2, fx, fc) + k * SUB, SUB) for fx, fc in KINDS], axis=0)

    def pairs(rows, bias, lowest, n):
        cols = slice(lowest * ROWS, (lowest + n) * ROWS)
        s = scores_of(rows, win[cols])
        best_win[:, cols] = jnp.maximum(best_win[:, cols], over_rows(add_rows_bias(s, bias)))
        return over_cols(s + live_cols[:, cols])

    def win_pairs(dz, lowest, n):
        own = slice(PLACE[dz] * ROWS, (PLACE[dz] + 1) * ROWS)
        best = pairs(win[own], row_bias(first_position(dz), ROWS), lowest, n)
        best_win[:, own] = jnp.maximum(best_win[:, own], turned(best))

    def far_pairs(k, lowest, n):
        best = pairs(far[k], far_bias(k), lowest, n)
        best_far_rows[k] = best if lowest == 0 else jnp.maximum(best_far_rows[k], best)

    def far_done(k):
        best = turned(best_far_rows[k])
        for kind in range(3):
            best_far[kind, :, k * SUB : (k + 1) * SUB] = best[:, kind * SUB : (kind + 1) * SUB]

    def large_self():
        own = slice(own_first, own_first + ROWS)
        s = scores_of(win[own], win[own])
        r = lax.broadcasted_iota(jnp.int32, s.shape, 0)
        q = lax.broadcasted_iota(jnp.int32, s.shape, 1)
        s = add_rows_bias(jnp.where(r == q, DEAD, s), row_bias(first_position(0), ROWS))
        best_win[:, own] = jnp.maximum(best_win[:, own], over_rows(s))

    def small_col_bias(meta_row, meta_col, first, n):
        at = first + lax.broadcasted_iota(jnp.int32, (1, n), 1)
        r = jnp.concatenate([meta_row[0:1]] * (n // 128), axis=1)
        q = jnp.concatenate([meta_col[0:1]] * (n // 128), axis=1)
        return jnp.where(((r >> 10) == (q >> 10)) & (at < (q & 1023)), 0.0, DEAD)

    def small_row_bias(meta_row, meta_col, first, n):
        at = first + lax.broadcasted_iota(jnp.int32, (n, 128), 0)
        r, q = meta_row[0:1], meta_col[0:1]
        live = jnp.where((r >> 10) == (q >> 10), r & 1023, 0)
        return jnp.where(at < live, 0.0, DEAD)

    def small_self():
        for f in range(0, BR, HALF):
            s = scores_of(near[1, f : f + HALF], near[1])
            r = f + lax.broadcasted_iota(jnp.int32, s.shape, 0)
            q = lax.broadcasted_iota(jnp.int32, s.shape, 1)
            bias = small_row_bias(meta[1], meta[1], f, HALF)
            s = add_rows_bias(jnp.where(r == q, DEAD, s), bias)
            best_near[1] = jnp.maximum(best_near[1], over_rows(s))

    def one_above():
        def step(h, carry):
            f = pl.multiple_of(h * HALF, HALF)
            s = scores_of(near[2, pl.ds(f, HALF)], near[1])
            rb = small_row_bias(meta[2], meta[1], f, HALF)
            cb = small_col_bias(meta[2], meta[1], 0, BR)
            best_near[1] = jnp.maximum(best_near[1], over_rows(add_rows_bias(s, rb)))
            best_near_rows[0, pl.ds(f, HALF)] = jnp.maximum(best_near_rows[0, pl.ds(f, HALF)], over_cols(s + cb))
            return carry

        lax.fori_loop(0, 2, step, 0)

    def two_apart():
        low = 1 - y // 2

        def step(h, carry):
            fr = pl.multiple_of((h * low + (1 - low)) * HALF, HALF)
            fc = pl.multiple_of(h * (1 - low) * HALF, HALF)
            s = scores_of(near[2, pl.ds(fr, HALF)], near[0, pl.ds(fc, HALF)])
            rb = small_row_bias(meta[2], meta[0], fr, HALF)
            cb = small_col_bias(meta[2], meta[0], fc, HALF)
            best_near[0, :, pl.ds(fc, HALF)] = jnp.maximum(
                best_near[0, :, pl.ds(fc, HALF)], over_rows(add_rows_bias(s, rb))
            )
            best_near_rows[0, pl.ds(fr, HALF)] = jnp.maximum(best_near_rows[0, pl.ds(fr, HALF)], over_cols(s + cb))
            return carry

        lax.fori_loop(0, 2, step, 0)

    def with_across(lowest, n):
        def step(j, carry):
            slot = lowest + j // 2
            f = pl.multiple_of(lax.rem(j, 2) * HALF, HALF)
            s = scores_of(across[pl.ds(f, HALF)], near[slot])
            rb = small_row_bias(meta_across[...], meta[slot], f, HALF)
            cb = small_col_bias(meta_across[...], meta[slot], 0, BR)
            best_near[slot] = jnp.maximum(best_near[slot], over_rows(add_rows_bias(s, rb)))
            best_near_rows[1, pl.ds(f, HALF)] = jnp.maximum(best_near_rows[1, pl.ds(f, HALF)], over_cols(s + cb))
            return carry

        lax.fori_loop(0, 2 * n, step, 0)

    def take(k):
        fwd_copy(1, k).wait_recv()
        cross_copy(k).start()
        sib_copy(k).start()

    def pass_on(k):
        cross_copy(k).wait_recv()
        diag_copy(k).start()

    def arrived(k):
        sib_copy(k).wait_recv()
        diag_copy(k).wait_recv()

    large_self()
    small_self()
    ends = [first + n for first, n in PIECES]
    halves_due = next(k for k in range(N_PIECE) if ends[k] >= 2 * SUB)
    for k in range(N_PIECE):
        for i in range(2):
            own_copy(i, k).wait_recv()
            if k == 0:
                first = PLACE[2 * i - 1] * ROWS
                piece = slice(first, first + PIECES[0][1])
                win[piece] = unit_rows(win[piece])
            fwd_copy(i, k).start()
        if k == halves_due:
            for i in range(2):
                near_copy(i, 0).wait_recv()
            for n in range(3):
                meta_copy(n).wait_recv()

            @pl.when(wide)
            def _():
                for i in range(2):
                    hop_copy(i).start()
                meta_copy(3).start()
                across_copy().wait_recv()
                with_across(1, 1)

    win_pairs(1, 1, 2)

    def small_first():
        for i in range(2):
            near_copy(i, 1).wait_recv()
        one_above()
        two_apart()

        @pl.when(wide)
        def _():
            with_across(0, 1)
            with_across(2, 1)

    def small_last():
        @pl.when(wide)
        def _():
            for i in range(2):
                hop_copy(i).wait_recv()
            meta_copy(3).wait_recv()
            with_across(3, 1)
            best_across[...] = turned(best_near_rows[1])

        best_near[2] = jnp.maximum(best_near[2], turned(best_near_rows[0]))
        for n in range(2):
            small_result(n).start()

        @pl.when(wide)
        def _():
            for n in (2, 3):
                small_result(n).start()

    seen = passed = 0
    for k in range(N_PIECE):
        take(k)
        if ends[k] <= 2 * SUB:
            while passed < k:
                pass_on(passed)
                passed += 1
        if ends[k] == SUB:
            small_first()
        if ends[k] == 2 * SUB:
            small_last()
        while seen < passed - 1:
            arrived(seen)
            seen += 1
            if ends[seen - 1] % SUB == 0:
                far_pairs(ends[seen - 1] // SUB - 1, 0, 3)
    while ends[passed] < ROWS:
        pass_on(passed)
        passed += 1
    while ends[seen] <= 2 * SUB:
        arrived(seen)
        seen += 1
        if ends[seen - 1] % SUB == 0:
            far_pairs(ends[seen - 1] // SUB - 1, 0, 3)
    pass_on(N_PIECE - 1)
    for k in range(N_PIECE):
        fwd_copy(0, k).wait_recv()
    win_pairs(2, 2, 2)
    far_pairs(0, 3, 2)
    far_done(0)
    far_pairs(1, 3, 2)
    far_done(1)
    for k in range(seen, N_PIECE):
        arrived(k)
    far_pairs(2, 0, 5)
    far_done(2)
    for n in (6, 5, 4, 0, 3, 1, 2):
        large_result(n).start()

    at = lax.broadcasted_iota(jnp.int32, (1, BR), 1)
    for n in range(3):
        small_result(n).wait_recv()
    best = best_near[1]
    for n in range(3):
        best = jnp.maximum(best, got_small[n])
    small_out[...] = jnp.where(at < small_count[0, 0], jnp.max(best, axis=0, keepdims=True), 0.0)
    for k in range(N_PIECE):
        for i in range(2):
            own_copy(i, k).wait_send()
            fwd_copy(i, k).wait_send()
        sib_copy(k).wait_send()
        cross_copy(k).wait_send()
        diag_copy(k).wait_send()
    for i in range(2):
        for h in range(2):
            near_copy(i, h).wait_send()
    for n in range(3):
        meta_copy(n).wait_send()
    for n in range(2):
        small_result(n).wait_send()

    @pl.when(wide)
    def _():
        for i in range(2):
            hop_copy(i).wait_send()
        meta_copy(3).wait_send()
        for n in (2, 3):
            small_result(n).wait_send()

    @pl.when(thin)
    def _():
        across_copy().wait_send()

    at = first_position(0) + lax.broadcasted_iota(jnp.int32, (1, ROWS), 1)
    for n in range(7):
        large_result(n).wait_recv()
    best = best_win[:, own_first : own_first + ROWS]
    for n in range(7):
        best = jnp.maximum(best, got_large[n])
    large_out[...] = jnp.where(at < count, jnp.max(best, axis=0, keepdims=True), 0.0)
    for n in range(7):
        large_result(n).wait_send()


def hand_out(large, small, large_out, small_out):
    large_out[...] = large[...].reshape(ROWS)
    small_out[...] = small[...].reshape(1, 1, BR)


def body(large_emb, large_count, small_emb, small_ids, small_count):
    vmem = pl.BlockSpec(memory_space=pltpu.VMEM)
    dma = pltpu.SemaphoreType.DMA
    f32, bf16, i32 = jnp.float32, jnp.bfloat16, jnp.int32
    large, small = pl.pallas_call(
        kernel,
        out_shape=(jax.ShapeDtypeStruct((1, ROWS), f32), jax.ShapeDtypeStruct((1, BR), f32)),
        in_specs=[pl.BlockSpec(memory_space=pl.ANY)] * 5,
        out_specs=(vmem, vmem),
        scratch_shapes=[
            pltpu.VMEM((ROWS, D), bf16),
            pltpu.VMEM((BR, D), bf16),
            pltpu.VMEM((5 * ROWS, D), bf16),
            pltpu.VMEM((ROWS // SUB, 3 * SUB, D), bf16),
            pltpu.VMEM((4, BR, D), bf16),
            pltpu.VMEM((BR, D), bf16),
            pltpu.VMEM((4, 8, 128), i32),
            pltpu.VMEM((8, 128), i32),
            pltpu.VMEM((1, 5 * ROWS), f32),
            pltpu.VMEM((8, 5 * ROWS), f32),
            pltpu.VMEM((ROWS // SUB, 3 * SUB, 128), f32),
            pltpu.VMEM((3, 8, ROWS), f32),
            pltpu.VMEM((4, 8, BR), f32),
            pltpu.VMEM((2, BR, 128), f32),
            pltpu.VMEM((8, BR), f32),
            pltpu.VMEM((7, 8, ROWS), f32),
            pltpu.VMEM((3, 8, BR), f32),
            pltpu.SMEM((1,), i32), pltpu.SMEM((1, 1), i32), pltpu.SMEM((1, 1), i32),
            dma((3,)), dma((3,)), dma((2, N_PIECE)), dma((2, N_PIECE)), dma((2, N_PIECE)), dma((2, N_PIECE)),
            dma((N_PIECE,)), dma((N_PIECE,)), dma((N_PIECE,)), dma((N_PIECE,)), dma((N_PIECE,)), dma((N_PIECE,)),
            dma((2, 2)), dma((2, 2)), dma((2,)), dma((2,)), dma((1,)), dma((1,)), dma((4,)), dma((4,)),
            dma((7,)), dma((7,)), dma((4,)), dma((3,)),
        ],
        compiler_params=pltpu.CompilerParams(
            collective_id=0, has_side_effects=True, vmem_limit_bytes=63_200_000
        ),
        name="cluster_maxima",
    )(large_count, small_ids, small_count, large_emb, small_emb.reshape(BR, D))
    return pl.pallas_call(
        hand_out,
        out_shape=(jax.ShapeDtypeStruct((ROWS,), f32), jax.ShapeDtypeStruct((1, 1, BR), f32)),
        in_specs=[vmem, vmem],
        out_specs=(vmem, vmem),
        name="hand_out",
    )(large, small)


def solution(mesh):
    placed = (
        P(("grp", "blk"), None),
        P("grp"),
        P("grp", "blk", None, None),
        P("grp", "blk"),
        P("grp", "blk"),
    )
    return jax.shard_map(
        body,
        mesh=mesh,
        in_specs=placed,
        out_specs=(P(("grp", "blk")), P("grp", "blk", None)),
        check_vma=False,
    )
```
